32 devices in a mesh: dp: 2 (over y), expert: 16 (over z, x, core).
Axes of the slice: x: 2, y: 2, z: 4, core: 2. Of those that a mesh axis runs over, the one named last changes fastest.
Arguments:
- inputs_one: bfloat16 [16, 64, 2048], P('expert'), may hold values from -3 to 3
- queries: bfloat16 [16, 64, 2048], P('expert'), may hold values from -14 to 14
- key_heads: bfloat16 [16, 64, 2048], P('expert'), may hold values from -14 to 14
- value_heads: bfloat16 [16, 64, 2048], P('expert'), may hold values from -6 to 6
- groups: int32 [16, 64], P('expert'), may hold values from 0 to 3, never falling along the last dimension, each value on 1 to 32 neighbouring positions
- inputs_two: bfloat16 [16, 64, 2048], P('expert'), may hold values from -3 to 3
- norm_gain: float32 [2048], replicated, may hold values from 0.1 to 1.9
- router: bfloat16 [2048, 64], replicated, may hold values from -0.125 to 0.125
- experts_old: bfloat16 [16, 1024, 3, 4, 2048], P('expert', 'dp'), may hold values from -0.1875 to 0.1875
- routes_one: int32 [16, 64, 8], P('expert'), may hold values from 0 to 63, all different within a row; in each aligned block of 64 rows (0 to 63, 64 to 127, ..., all dimensions but the last counted through in order) at most 16 rows name the same one
- routes_two: int32 [16, 64, 8], P('expert'), may hold values from 0 to 63, all different within a row; in each aligned block of 64 rows (0 to 63, 64 to 127, ..., all dimensions but the last counted through in order) at most 16 rows name the same one
- old_slots: int32 [64], replicated, may hold values from 0 to 63, each once
- new_slots: int32 [80], replicated, may hold values from 0 to 63, as said below
Outputs:
- output_one: bfloat16 [16, 64, 2048], P('expert', 'dp')
- output_two: bfloat16 [16, 64, 2048], P('expert', 'dp')
- experts_new: bfloat16 [16, 1024, 3, 5, 2048], P('expert', 'dp')
The draws below stay inside these ranges and needn't reach their ends.
Inputs may be any that keep to these rules, and one draw needn't show every extreme that they name: `routes_one`: among the 8 entries of a token no expert repeats, and among the routes of one expert index's 64 tokens no expert is named more than 16 times. `routes_two`: among the 8 entries of a token no expert repeats, and among the routes of one expert index's 64 tokens no expert is named more than 16 times. `groups`: group numbers never fall along a row; each group has 1 to 32 tokens. `old_slots`: each expert fills exactly one slot; slot s of expert index j is entry j * 4 + s. `new_slots`: each expert fills one or two slots, and some fill two; slot s of expert index j is entry j * 5 + s.
All inputs are finite; a program needn't handle non-finite values.
Results may differ from the reference program's by a relative error of at most 0.0062.
Values may be sent and summed in bfloat16 or wider, within the bound.
A program may use at most 192 MiB of HBM per device.

```python
import math
import jax
import jax.numpy as jnp
import numpy as np
from jax import lax

D = 2048
HEADS = 16
HEAD_DIM = 128
EXPERTS = 64
FF = 1024
TOPK = 8
COL_TOK = 64
GROUPS = 4
MOST = 16
SEG_MOST = 32
SLOTS_OLD = 4
SLOTS_NEW = 5
N_DP = 2
N_EXPERT = 16


def attention_pair(key):
    shape = (EXPERTS // SLOTS_OLD, COL_TOK, HEADS * HEAD_DIM)
    base = jnp.clip(jax.random.normal(jax.random.fold_in(key, 101), shape, jnp.float32), -6.0, 6.0)
    other = jnp.clip(jax.random.normal(jax.random.fold_in(key, 102), shape, jnp.float32), -6.0, 6.0)
    return (other, base)


def draw_queries(key, part):
    return attention_pair(key)[0].astype(jnp.bfloat16)


def draw_key_heads(key, part):
    return attention_pair(key)[1].astype(jnp.bfloat16)


def draw_new_slots(key, part):
    primary = jax.random.permutation(jax.random.fold_in(key, 201), EXPERTS)
    extras = jax.random.permutation(jax.random.fold_in(key, 202), EXPERTS)[:EXPERTS // SLOTS_OLD]
    joined = jnp.concatenate([primary, extras]).astype(jnp.int32)
    return jax.random.permutation(jax.random.fold_in(key, 203), joined).astype(jnp.int32)


def levels(own_key, extent, cuts, least, high):
    loudness = 1.0
    for dim, shards_of in cuts:
        draws = jax.random.uniform(jax.random.fold_in(jax.random.fold_in(own_key, 6), dim), (shards_of,), jnp.float32, least / len(cuts), high / len(cuts))
        loudness = loudness * jnp.repeat(jnp.exp(draws), extent[dim] // shards_of).reshape((-1,) + (1,) * (len(extent) - 1 - dim))
    return loudness


def split_up(count, total, reach, lean):
    portions = [(1 << 20) // math.isqrt(rank ** lean) + 1 for rank in range(2, count + 1)]
    rest, given = total - reach - (count - 1), [1] * (count - 1)
    while rest > 0:
        candidates = [i for i in range(count - 1) if given[i] < reach]
        whole, left = sum([portions[i] for i in candidates]), rest
        for i in candidates:
            more = min(reach - given[i], max(1, left * portions[i] // whole), rest)
            given[i] = given[i] + more
            rest = rest - more
    return np.array([reach] + given)


def uneven(stream_key, count, total, reach, slope):
    if count == 2:
        one = jax.random.randint(stream_key, (), max(1, total - reach), min(reach, total - 1) + 1)
        return jnp.stack([one, total - one])
    sizes = jnp.asarray(split_up(count, total, reach, slope), jnp.int32)
    twos = (count - 1) // 2
    donor, sink = sizes[1:1 + 2 * twos:2], sizes[2:2 + 2 * twos:2]
    room = jnp.minimum(donor - 1, reach - sink)
    shifted = jax.random.randint(jax.random.fold_in(stream_key, 1), (twos,), 0, 1 << 20) % (room + 1)
    sizes = sizes.at[1:1 + 2 * twos:2].set(donor - shifted).at[2:2 + 2 * twos:2].set(sink + shifted)
    return sizes[jax.random.permutation(jax.random.fold_in(stream_key, 2), count)]


def deal_out(stream_key, own, number, rows, number_of, top, most, skew):
    sequence = jax.random.permutation(stream_key, number_of)
    crowded, ordinary = shares(number_of, rows * top, most, skew, True), shares(number_of, rows * top, most, skew, False)
    places = jnp.arange(number_of)

    def named(sizes, turn):
        used = int((sizes > 0).sum())
        fixed = max(1, used // 4)
        shifted = fixed + (places - fixed + turn * (used - fixed)) % max(1, number_of - fixed)
        return jnp.zeros((number_of,), jnp.int32).at[sequence[jnp.where(places < fixed, places, shifted)]].set(jnp.asarray(sizes, jnp.int32))

    sizes = jnp.where(number % 4 == 0, named(crowded, number // 4), named(ordinary, number - number // 4 - 1))
    mixed = jax.random.permutation(jax.random.fold_in(own, 3), number_of)
    giver, receiver = mixed[0:number_of // 2 * 2:2], mixed[1:number_of // 2 * 2:2]
    room = jnp.minimum(sizes[giver] - 1, most - sizes[receiver]) // 2
    room = jnp.where((giver == sequence[0]) | (receiver == sequence[0]) | (sizes[receiver] == 0), 0, jnp.maximum(room, 0))
    shifted = jax.random.randint(jax.random.fold_in(own, 4), (number_of // 2,), 0, 1 << 20) % (room + 1)
    sizes = sizes.at[giver].add(-shifted).at[receiver].add(shifted)
    members = jnp.searchsorted(jnp.cumsum(sizes), jnp.arange(rows * top), side="right").astype(jnp.int32)
    listing = members.reshape(top, rows).T
    listing = listing[jax.random.permutation(jax.random.fold_in(own, 1), rows)]
    turn = jax.random.randint(jax.random.fold_in(own, 2), (rows, 1), 0, top)
    return jnp.take_along_axis(listing, (jnp.arange(top)[None, :] + turn) % top, axis=1)


def shares(number_of, total, limit, skew, full):
    portions = [(1 << 20) // math.isqrt(rank ** skew) + 1 for rank in range(1, number_of + 1)]
    largest = limit if full else min(limit, max(-(-total // number_of), total * portions[0] // sum(portions)))
    least = 1 if total - largest >= number_of - 1 else 0
    given, spare = [largest] + [least] * (number_of - 1), total - largest - least * (number_of - 1)
    while spare > 0:
        candidates = [i for i in range(1, number_of) if given[i] < largest] or [i for i in range(1, number_of) if given[i] < limit]
        whole, left = sum([portions[i] for i in candidates]), spare
        for i in candidates:
            more = min(limit - given[i], max(1, left * portions[i] // whole), spare)
            given[i] = given[i] + more
            spare = spare - more
    return np.array(given)


def bell_draw(own_key, shape, width, bound, shards=(), held_as=jnp.bfloat16):
    drawn = jax.random.normal(own_key, shape, jnp.float32) * width
    if len(shards) > 0:
        drawn = levels(own_key, shape, shards, -0.22, 0.18) * drawn
    return jnp.clip(drawn, min=-bound, max=bound).astype(held_as)


def setup_inputs(seed: int = 0) -> dict:
    keys = jax.random.split(jax.random.key(seed), 14)
    inputs_one = bell_draw(keys[0], (N_EXPERT, COL_TOK, D), 0.5, 3.0, ((0, 16),))
    queries = draw_queries(jax.random.fold_in(keys[13], 71), 0)
    key_heads = draw_key_heads(jax.random.fold_in(keys[13], 71), 0)
    value_heads = bell_draw(keys[3], (N_EXPERT, COL_TOK, D), 1.0, 6.0, ((0, 16),))
    groups = jax.vmap(lambda own: jnp.searchsorted(jnp.cumsum(uneven(own, GROUPS, COL_TOK, SEG_MOST, 2)), jnp.arange(COL_TOK), side="right"))(jax.random.split(keys[4], N_EXPERT)).reshape((N_EXPERT, COL_TOK)).astype(jnp.int32)
    inputs_two = bell_draw(keys[5], (N_EXPERT, COL_TOK, D), 0.5, 3.0, ((0, 16),))
    norm_gain = jnp.clip(1.0 + 0.18 * jax.random.normal(keys[6], (D,), jnp.float32), 0.1, 1.9)
    router = bell_draw(keys[7], (D, EXPERTS), D ** -0.5, 0.125)
    experts_old = bell_draw(keys[8], (N_EXPERT, FF, 3, SLOTS_OLD, D), (D // 2) ** -0.5, 0.1875, ((0, 16), (1, 2)))
    routes_one_keys = jax.random.split(jax.random.fold_in(keys[9], 1), N_EXPERT * COL_TOK // COL_TOK)
    routes_one_turns = jax.random.permutation(jax.random.fold_in(keys[9], 3), N_EXPERT * COL_TOK // COL_TOK)
    routes_one = jax.vmap(lambda own, number: deal_out(jax.random.fold_in(keys[9], 2), own, number, COL_TOK, EXPERTS, TOPK, MOST, 1))(routes_one_keys, routes_one_turns).reshape((N_EXPERT, COL_TOK, TOPK))
    routes_two_keys = jax.random.split(jax.random.fold_in(keys[10], 1), N_EXPERT * COL_TOK // COL_TOK)
    routes_two_turns = jax.random.permutation(jax.random.fold_in(keys[10], 3), N_EXPERT * COL_TOK // COL_TOK)
    routes_two = jax.vmap(lambda own, number: deal_out(jax.random.fold_in(keys[10], 2), own, number, COL_TOK, EXPERTS, TOPK, MOST, 1))(routes_two_keys, routes_two_turns).reshape((N_EXPERT, COL_TOK, TOPK))
    old_slots = jax.random.permutation(keys[11], EXPERTS).astype(jnp.int32)
    new_slots = draw_new_slots(jax.random.fold_in(keys[13], 71), 0)
    return dict(inputs_one=inputs_one, queries=queries, key_heads=key_heads, value_heads=value_heads, groups=groups, inputs_two=inputs_two, norm_gain=norm_gain, router=router, experts_old=experts_old, routes_one=routes_one, routes_two=routes_two, old_slots=old_slots, new_slots=new_slots)


EPS = 1e-06
MASKED = -1e+30

def attention(queries, key_heads, value_heads, groups):
    shape = (N_EXPERT, COL_TOK, HEADS, HEAD_DIM)
    query_f = queries.astype(jnp.float32).reshape(shape)
    key_f = key_heads.astype(jnp.float32).reshape(shape)
    value_f = value_heads.astype(jnp.float32).reshape(shape)
    scores = jnp.einsum('jthd,juhd->jhtu', query_f, key_f) * HEAD_DIM ** (-0.5)
    allowed = (groups[:, :, None] == groups[:, None, :])[:, None]
    scores = jnp.where(allowed, scores, MASKED)
    row_max = lax.optimization_barrier(jnp.max(scores, -1, keepdims=True))
    expo = jnp.exp(scores - row_max)
    attn_probs = (expo / lax.optimization_barrier(jnp.sum(expo, -1, keepdims=True))).astype(jnp.bfloat16)
    context = jnp.einsum('jhtu,juhd->jthd', attn_probs.astype(jnp.float32), value_f)
    return context.reshape(N_EXPERT, COL_TOK, D)

def rms_norm(hidden, norm_gain):
    scale = lax.rsqrt(lax.optimization_barrier(jnp.mean(hidden * hidden, -1, keepdims=True)) + EPS)
    return (hidden * scale * norm_gain).astype(jnp.bfloat16)

def mixture(normed, routes, router, gate_w, up_w, down_w):
    logits = jnp.dot(normed.reshape(-1, D), router, preferred_element_type=jnp.float32)
    logits = logits.reshape(N_EXPERT, COL_TOK, EXPERTS)
    chosen = jnp.take_along_axis(logits, routes, -1)
    sig = jax.nn.sigmoid(chosen)
    gates = sig / lax.optimization_barrier(jnp.sum(sig, -1, keepdims=True))
    route_total = COL_TOK * TOPK
    down_split = down_w.reshape(EXPERTS, N_DP, FF // N_DP, D)

    def column(item):
        rows, route, gate = item
        flat = route.reshape(-1)
        onehot = (flat[:, None] == jnp.arange(EXPERTS, dtype=jnp.int32)[None, :]).astype(jnp.int32)
        rank = lax.optimization_barrier(jnp.sum((jnp.cumsum(onehot, 0) - 1) * onehot, 1))
        place = flat * MOST + rank
        source = jnp.full((EXPERTS * MOST,), route_total, jnp.int32)
        source = source.at[place].set(jnp.arange(route_total, dtype=jnp.int32))
        valid = source < route_total
        token = jnp.minimum(source // TOPK, COL_TOK - 1)
        batch = jnp.where(valid[:, None], rows[token].astype(jnp.float32), 0.0).reshape(EXPERTS, MOST, D)
        first = jnp.einsum('emd,efd->emf', batch, gate_w)
        second = jnp.einsum('emd,efd->emf', batch, up_w)
        act = (jax.nn.silu(first) * second).astype(jnp.bfloat16)
        pieces = act.astype(jnp.float32).reshape(EXPERTS, MOST, N_DP, FF // N_DP)
        partial_value = jnp.einsum('emsf,esfd->emsd', pieces, down_split)
        partial_value = lax.optimization_barrier(partial_value.astype(jnp.bfloat16)).astype(jnp.float32)
        partial_value = lax.optimization_barrier(jnp.sum(partial_value, 2)).reshape(EXPERTS * MOST, D)
        picked = partial_value[place].reshape(COL_TOK, TOPK, D)
        return lax.optimization_barrier(jnp.sum(picked * gate[:, :, None], 1))
    return lax.map(column, (normed, routes, gates))

def reference(inputs_one, queries, key_heads, value_heads, groups, inputs_two, norm_gain, router, experts_old, routes_one, routes_two, old_slots, new_slots):
    context = attention(queries, key_heads, value_heads, groups)
    hidden_one = inputs_one.astype(jnp.float32) + context
    hidden_two = inputs_two.astype(jnp.float32)
    flat_old = jnp.moveaxis(experts_old, 3, 1).reshape(N_EXPERT * SLOTS_OLD, FF, 3, D)
    position = jnp.zeros((EXPERTS,), jnp.int32).at[old_slots].set(jnp.arange(EXPERTS, dtype=jnp.int32))
    table = flat_old[position]
    gate_w = table[:, :, 0].astype(jnp.float32)
    up_w = table[:, :, 1].astype(jnp.float32)
    down_w = table[:, :, 2].astype(jnp.float32)
    mixed_one = mixture(rms_norm(hidden_one, norm_gain), routes_one, router, gate_w, up_w, down_w)
    mixed_two = mixture(rms_norm(hidden_two, norm_gain), routes_two, router, gate_w, up_w, down_w)
    output_one = (hidden_one + mixed_one).astype(jnp.bfloat16)
    output_two = (hidden_two + mixed_two).astype(jnp.bfloat16)
    experts_new = table[new_slots].reshape(N_EXPERT, SLOTS_NEW, FF, 3, D)
    experts_new = jnp.transpose(experts_new, (0, 2, 3, 1, 4))
    return (output_one, output_two, experts_new)
```

```python
import jax
import jax.numpy as jnp
from jax import lax
from jax.sharding import PartitionSpec as P

D = 2048
HEADS = 16
HEAD_DIM = 128
EXPERTS = 64


EPS = 1e-06
MASKED = -1e30


def rms_norm(hidden, norm_gain):
    scale = lax.rsqrt(jnp.mean(hidden * hidden, -1, keepdims=True) + EPS)
    return (hidden * scale * norm_gain).astype(jnp.bfloat16)


def shards(
    inputs_one,
    queries,
    key_heads,
    value_heads,
    groups,
    inputs_two,
    norm_gain,
    router,
    experts_old,
    routes_one,
    routes_two,
    old_slots,
    new_slots,
):
    index_count = lax.axis_size("expert")
    slice_count = lax.axis_size("dp")
    weights_local = experts_old[0]
    hidden_rows = weights_local.shape[0]
    old_width = weights_local.shape[2]
    piece_rows = hidden_rows // index_count
    new_total = new_slots.shape[0]
    new_width = new_total // index_count
    old_total = old_slots.shape[0]
    column = inputs_one.shape[1]
    own_rows = column // slice_count
    moving = jnp.transpose(
        weights_local.reshape(index_count, piece_rows, 3, old_width, D), (0, 2, 3, 1, 4)
    )
    spread = lax.all_to_all(moving, "expert", split_axis=0, concat_axis=0, tiled=True)
    shape = (column, HEADS, HEAD_DIM)
    scores = jnp.einsum(
        "thd,uhd->htu",
        queries[0].reshape(shape),
        key_heads[0].reshape(shape),
        preferred_element_type=jnp.float32,
    ) * HEAD_DIM ** (-0.5)
    allowed = groups[0][:, None] == groups[0][None, :]
    scores = jnp.where(allowed[None], scores, MASKED)
    row_max = jnp.max(scores, -1, keepdims=True)
    expo = jnp.exp(scores - row_max)
    attn_probs = (expo / jnp.sum(expo, -1, keepdims=True)).astype(jnp.bfloat16)
    context = jnp.einsum(
        "htu,uhd->thd",
        attn_probs,
        value_heads[0].reshape(shape),
        preferred_element_type=jnp.float32,
    ).reshape(column, D)
    hidden_one = inputs_one[0].astype(jnp.float32) + context
    hidden_two = inputs_two[0].astype(jnp.float32)
    normed_one = rms_norm(hidden_one, norm_gain)
    normed_two = rms_norm(hidden_two, norm_gain)
    expert_ids = jnp.arange(EXPERTS, dtype=jnp.int32)
    old_ids = jnp.arange(old_total, dtype=jnp.int32)
    old_place = jnp.sum(
        jnp.where(old_slots[None, :] == expert_ids[:, None], old_ids[None, :], 0), 1
    )

    def slot_gates(normed, routes):
        logits = jnp.dot(normed, router, preferred_element_type=jnp.float32)
        chosen_hot = routes[:, :, None] == expert_ids[None, None, :]
        picked = jnp.where(jnp.any(chosen_hot, 1), jax.nn.sigmoid(logits), 0.0)
        gates = picked / jnp.sum(picked, -1, keepdims=True)
        slot_hot = (old_slots[None, :] == expert_ids[:, None]).astype(jnp.float32)
        return jnp.dot(gates, slot_hot, precision=lax.Precision.HIGHEST)

    def side_by_side(one, two):
        split = (slice_count, 1, own_rows, one.shape[-1])
        return jnp.concatenate([one.reshape(split), two.reshape(split)], 1).reshape(
            2 * column, one.shape[-1]
        )

    gates = side_by_side(
        slot_gates(normed_one, routes_one[0]), slot_gates(normed_two, routes_two[0])
    )
    tokens = lax.all_gather(side_by_side(normed_one, normed_two), "expert", tiled=True)
    own_gates = lax.all_to_all(
        jnp.moveaxis(gates.reshape(2 * column, index_count, old_width), 1, 0),
        "expert",
        split_axis=0,
        concat_axis=0,
        tiled=True,
    ).reshape(index_count * 2 * column, old_width)
    first = jnp.einsum("td,nsfd->tnsf", tokens, moving[:, 0], preferred_element_type=jnp.float32)
    second = jnp.einsum("td,nsfd->tnsf", tokens, moving[:, 1], preferred_element_type=jnp.float32)
    act = (jax.nn.silu(first) * second * own_gates[:, None, :, None]).astype(jnp.bfloat16)
    mixed = jnp.einsum("tnsf,nsfd->td", act, moving[:, 2], preferred_element_type=jnp.float32)
    spread, mixed = lax.optimization_barrier((spread, mixed))
    summed = lax.psum_scatter(mixed, ("expert", "dp"), scatter_dimension=0, tiled=True)
    summed = summed.reshape(2, own_rows, D)
    start = lax.axis_index("dp") * own_rows
    own_one = lax.dynamic_slice_in_dim(hidden_one, start, own_rows, 0)
    own_two = lax.dynamic_slice_in_dim(hidden_two, start, own_rows, 0)
    output_one = (own_one + summed[0]).astype(jnp.bfloat16)[None]
    output_two = (own_two + summed[1]).astype(jnp.bfloat16)[None]

    table = jnp.moveaxis(spread, 2, 1).reshape(index_count * old_width, 3, piece_rows, D)
    new_place = jnp.sum(
        jnp.where(new_slots[:, None] == expert_ids[None, :], old_place[None, :], 0), 1
    )
    outgoing = table[new_place].reshape(index_count, new_width, 3, piece_rows, D)
    arrived = lax.all_to_all(outgoing, "expert", split_axis=0, concat_axis=0, tiled=True)
    weights_new = jnp.transpose(arrived, (0, 3, 2, 1, 4)).reshape(hidden_rows, 3, new_width, D)
    return (output_one, output_two, weights_new[None])


def solution(mesh):
    in_specs = (
        P("expert", None, None),
        P("expert", None, None),
        P("expert", None, None),
        P("expert", None, None),
        P("expert", None),
        P("expert", None, None),
        P(),
        P(),
        P("expert", "dp", None, None, None),
        P("expert", None, None),
        P("expert", None, None),
        P(),
        P(),
    )
    out_specs = (
        P("expert", "dp", None),
        P("expert", "dp", None),
        P("expert", "dp", None, None, None),
    )
    return jax.shard_map(shards, mesh=mesh, in_specs=in_specs, out_specs=out_specs, check_vma=False)
```

```python
import jax
import jax.numpy as jnp
from jax import lax
from jax.sharding import PartitionSpec as P

D = 2048
HEADS = 16
HEAD_DIM = 128
EXPERTS = 64


EPS = 1e-06
MASKED = -1e30


def rms_norm(hidden, norm_gain):
    scale = lax.rsqrt(jnp.mean(hidden * hidden, -1, keepdims=True) + EPS)
    return (hidden * scale * norm_gain).astype(jnp.bfloat16)


def shards(
    inputs_one,
    queries,
    key_heads,
    value_heads,
    groups,
    inputs_two,
    norm_gain,
    router,
    experts_old,
    routes_one,
    routes_two,
    old_slots,
    new_slots,
):
    index_count = lax.axis_size("expert")
    slice_count = lax.axis_size("dp")
    weights_local = experts_old[0]
    hidden_rows = weights_local.shape[0]
    old_width = weights_local.shape[2]
    piece_rows = hidden_rows // index_count
    new_total = new_slots.shape[0]
    new_width = new_total // index_count
    old_total = old_slots.shape[0]
    column = inputs_one.shape[1]
    own_rows = column // slice_count
    parts = 2 if piece_rows % 2 == 0 else 1
    part_rows = piece_rows // parts
    pieces = weights_local.reshape(index_count, parts, part_rows, 3, old_width, D)
    spreads = [
        lax.all_to_all(
            jnp.transpose(pieces[:, part], (0, 2, 3, 1, 4)),
            "expert",
            split_axis=0,
            concat_axis=0,
            tiled=True,
        )
        for part in range(parts)
    ]
    shape = (column, HEADS, HEAD_DIM)
    scores = jnp.einsum(
        "thd,uhd->htu",
        queries[0].reshape(shape),
        key_heads[0].reshape(shape),
        preferred_element_type=jnp.float32,
    ) * HEAD_DIM ** (-0.5)
    allowed = groups[0][:, None] == groups[0][None, :]
    scores = jnp.where(allowed[None], scores, MASKED)
    row_max = jnp.max(scores, -1, keepdims=True)
    expo = jnp.exp(scores - row_max)
    attn_probs = (expo / jnp.sum(expo, -1, keepdims=True)).astype(jnp.bfloat16)
    context = jnp.einsum(
        "htu,uhd->thd",
        attn_probs,
        value_heads[0].reshape(shape),
        preferred_element_type=jnp.float32,
    ).reshape(column, D)
    hidden_one = inputs_one[0].astype(jnp.float32) + context
    hidden_two = inputs_two[0].astype(jnp.float32)
    normed_one = rms_norm(hidden_one, norm_gain)
    normed_two = rms_norm(hidden_two, norm_gain)
    expert_ids = jnp.arange(EXPERTS, dtype=jnp.int32)
    old_ids = jnp.arange(old_total, dtype=jnp.int32)
    old_place = jnp.sum(
        jnp.where(old_slots[None, :] == expert_ids[:, None], old_ids[None, :], 0), 1
    )

    def slot_gates(normed, routes):
        logits = jnp.dot(normed, router, preferred_element_type=jnp.float32)
        chosen_hot = routes[:, :, None] == expert_ids[None, None, :]
        picked = jnp.where(jnp.any(chosen_hot, 1), jax.nn.sigmoid(logits), 0.0)
        gates = picked / jnp.sum(picked, -1, keepdims=True)
        slot_hot = (old_slots[None, :] == expert_ids[:, None]).astype(jnp.float32)
        return jnp.dot(gates, slot_hot, precision=lax.Precision.HIGHEST)

    start = lax.axis_index("dp") * own_rows

    def own_share(one, two):
        return jnp.concatenate(
            [lax.dynamic_slice_in_dim(part, start, own_rows, 0) for part in (one, two)], 0
        )

    def gather_all(share):
        return lax.all_gather(
            lax.all_gather(share, "expert", tiled=True), "dp", tiled=True
        )

    tokens = gather_all(own_share(normed_one, normed_two))
    gates = gather_all(
        own_share(slot_gates(normed_one, routes_one[0]), slot_gates(normed_two, routes_two[0]))
    )
    own_gates = lax.dynamic_slice_in_dim(
        gates, lax.axis_index("expert") * old_width, old_width, 1
    )
    first = jnp.einsum(
        "td,fsd->tsf", tokens, weights_local[:, 0], preferred_element_type=jnp.float32
    )
    second = jnp.einsum(
        "td,fsd->tsf", tokens, weights_local[:, 1], preferred_element_type=jnp.float32
    )
    act = (jax.nn.silu(first) * second * own_gates[:, :, None]).astype(jnp.bfloat16)
    mixed = jnp.einsum(
        "tsf,fsd->td", act, weights_local[:, 2], preferred_element_type=jnp.float32
    )
    summed = lax.psum_scatter(mixed, "dp", scatter_dimension=0, tiled=True)
    summed = lax.psum_scatter(summed, "expert", scatter_dimension=0, tiled=True)
    outputs = (own_share(hidden_one, hidden_two) + summed).astype(jnp.bfloat16)
    output_one = outputs[None, :own_rows]
    output_two = outputs[None, own_rows:]

    new_place = jnp.sum(
        jnp.where(new_slots[:, None] == expert_ids[None, :], old_place[None, :], 0), 1
    )
    weights_new = jnp.zeros(
        (3, new_width, index_count, parts, part_rows, D), weights_local.dtype
    )
    for part in range(parts):
        table = jnp.moveaxis(spreads[part], 2, 1).reshape(
            index_count * old_width, 3, part_rows, D
        )
        outgoing = table[new_place].reshape(index_count, new_width, 3, part_rows, D)
        arrived = lax.all_to_all(outgoing, "expert", split_axis=0, concat_axis=0, tiled=True)
        weights_new = lax.optimization_barrier(
            weights_new.at[:, :, :, part].set(jnp.transpose(arrived, (2, 1, 0, 3, 4)))
        )
    weights_new = weights_new.reshape(3, new_width, hidden_rows, D)
    weights_new = jnp.transpose(weights_new, (2, 0, 1, 3))
    return (output_one, output_two, weights_new[None])


def solution(mesh):
    in_specs = (
        P("expert", None, None),
        P("expert", None, None),
        P("expert", None, None),
        P("expert", None, None),
        P("expert", None),
        P("expert", None, None),
        P(),
        P(),
        P("expert", "dp", None, None, None),
        P("expert", None, None),
        P("expert", None, None),
        P(),
        P(),
    )
    out_specs = (
        P("expert", "dp", None),
        P("expert", "dp", None),
        P("expert", "dp", None, None, None),
    )
    return jax.shard_map(shards, mesh=mesh, in_specs=in_specs, out_specs=out_specs, check_vma=False)
```
